32 devices in a mesh: seq: 16 (over z, x, core), head: 2 (over y).
Axes of the slice: x: 2, y: 2, z: 4, core: 2. Of those that a mesh axis runs over, the one named last changes fastest.
Arguments:
- queries: bfloat16 [8192, 4096], P(('seq', 'head')), may hold values from -5 to 5
- new_keys: bfloat16 [8192, 1024], P(('seq', 'head')), may hold values from -12 to 12
- new_values: bfloat16 [8192, 1024], P(('seq', 'head')), may hold values from -6 to 6
- cache_keys: bfloat16 [32768, 1024], P('seq', 'head'), may hold values from -12 to 12
- cache_values: bfloat16 [32768, 1024], P('seq', 'head'), may hold values from -6 to 6
- tile_lists: int32 [64, 8, 12], P('seq', 'head'), may hold values from 0 to 255, as said below
Outputs:
- attended: bfloat16 [8192, 4096], P(('seq', 'head'))
The draws below stay inside these ranges and needn't reach their ends.
Inputs may be any that keep to these rules, and one draw needn't show every extreme that they name: `tile_lists`: for one key head, the 12 tiles of one block's list are distinct; the lists of the 4 blocks of one index of seq together name exactly 24 distinct tiles, at most 2 of them of one index of seq (tiles k * 16 to k * 16 + 15), and some index has exactly 2.
All inputs are finite; a program needn't handle non-finite values.
Results may differ from the reference program's by a relative error of at most 0.003.
Values may be sent and summed in bfloat16 or wider, within the bound.
No kernel may reach another device: no remote copies, remote signals or barrier semaphores. Data moves between devices by JAX's collectives and lax.ppermute only.
A program may use at most 192 MiB of HBM per device.

```python
import math
import jax
import jax.numpy as jnp
from jax import lax

HQ = 32
KV = 8
HD = 128
QB = 128
TILE = 128
SEL = 12
NQB_DEV = 4
TILES_DEV = 16
POOL = 24
CAP = 2
PROMPT = 8192
CTX = 32768
NQB = 64
N_SEQ = 16


def one_group(group_key):
    slot_count = N_SEQ * CAP
    owner_of = jnp.arange(slot_count) // CAP
    rank_of = jnp.arange(slot_count) % CAP
    order_key, force_key, offset_key, mix_key = jax.random.split(group_key, 4)
    shuffle = jax.random.permutation(order_key, slot_count)
    forced = jax.random.randint(force_key, (), 0, N_SEQ)
    slot_score = jnp.where(owner_of == forced, rank_of - CAP, shuffle)
    ordering = jnp.argsort(slot_score, stable=True)[:POOL]
    offsets = jax.random.randint(offset_key, (N_SEQ,), 0, TILES_DEV)
    picked_owner = owner_of[ordering]
    picked_rank = rank_of[ordering]
    pool_ids = picked_owner * TILES_DEV + (offsets[picked_owner] + picked_rank) % TILES_DEV
    pool_ids = pool_ids[jax.random.permutation(mix_key, POOL)]
    position = (jnp.arange(NQB_DEV)[:, None] * SEL + jnp.arange(SEL)[None, :]) % POOL
    return pool_ids[position].astype(jnp.int32)


def draw_tile_lists(key, part):
    group_keys = jax.random.split(key, N_SEQ * KV)
    grouped = jax.vmap(one_group)(group_keys).reshape(N_SEQ, KV, NQB_DEV, SEL)
    return jnp.transpose(grouped, (0, 2, 1, 3)).reshape(NQB, KV, SEL)


def draw_queries(key, part):
    values = jax.random.truncated_normal(jax.random.fold_in(key, 1), -5.0, 5.0, (PROMPT, HQ * HD))
    return values.astype(jnp.float32).astype(jnp.bfloat16)


def draw_new_keys(key, part):
    values = 2.5 * jax.random.truncated_normal(jax.random.fold_in(key, 2), -4.8, 4.8, (PROMPT, KV * HD))
    return values.astype(jnp.float32).astype(jnp.bfloat16)


def block_levels(key, shape, cuts, smallest, high):
    def one(axis_at, shards_of):
        heights = jax.random.uniform(jax.random.fold_in(jax.random.fold_in(key, 6), axis_at), (shards_of,), jnp.float32, smallest / len(cuts), high / len(cuts))
        return jnp.repeat(jnp.exp(heights), shape[axis_at] // shards_of).reshape((-1,) + (1,) * (len(shape) - axis_at - 1))

    level = one(*cuts[0])
    for cut in cuts[1:]:
        level = level * one(*cut)
    return level


def noise(own_key, extent, spread, limit, pieces=(), kind=jnp.bfloat16):
    values = jax.random.normal(own_key, extent, jnp.float32) * spread
    if len(pieces) > 0:
        values = block_levels(own_key, extent, pieces, -0.22, 0.18) * values
    return jnp.clip(values, min=-limit, max=limit).astype(kind)


def setup_inputs(seed: int = 0) -> dict:
    key_list = jax.random.split(jax.random.key(seed), 7)
    queries = draw_queries(jax.random.fold_in(key_list[6], 71), 0)
    new_keys = draw_new_keys(jax.random.fold_in(key_list[6], 71), 0)
    new_values = noise(key_list[2], (PROMPT, KV * HD), 1.0, 6.0, ((0, 32),))
    cache_keys = noise(key_list[3], (CTX, KV * HD), 2.5, 12.0, ((0, 16), (1, 2)))
    cache_values = noise(key_list[4], (CTX, KV * HD), 1.0, 6.0, ((0, 16), (1, 2)))
    tile_lists = draw_tile_lists(jax.random.fold_in(key_list[6], 71), 0)
    return dict(queries=queries, new_keys=new_keys, new_values=new_values, cache_keys=cache_keys, cache_values=cache_values, tile_lists=tile_lists)


NEG_FILL = -1e+30

def reference(queries, new_keys, new_values, cache_keys, cache_values, tile_lists):
    group_size = HQ // KV
    scale_factor = 1.0 / math.sqrt(HD)
    query_blocks = queries.reshape(NQB, QB, KV, group_size, HD)
    key_blocks = new_keys.reshape(NQB, QB, KV, HD)
    value_blocks = new_values.reshape(NQB, QB, KV, HD)
    key_tiles = cache_keys.reshape(CTX // TILE, TILE, KV, HD)
    value_tiles = cache_values.reshape(CTX // TILE, TILE, KV, HD)
    head_pick = jnp.arange(KV)[:, None]
    causal = jnp.arange(QB)[:, None] >= jnp.arange(QB)[None, :]

    def one_block(block_index):
        query_block = query_blocks[block_index].astype(jnp.float32)
        chosen = tile_lists[block_index]
        earlier = jnp.maximum(block_index - 1, 0)
        context_keys = key_tiles[chosen, :, head_pick].reshape(KV, SEL * TILE, HD)
        context_values = value_tiles[chosen, :, head_pick].reshape(KV, SEL * TILE, HD)
        all_keys = jnp.concatenate([context_keys, jnp.transpose(key_blocks[earlier], (1, 0, 2)), jnp.transpose(key_blocks[block_index], (1, 0, 2))], axis=1).astype(jnp.float32)
        all_values = jnp.concatenate([context_values, jnp.transpose(value_blocks[earlier], (1, 0, 2)), jnp.transpose(value_blocks[block_index], (1, 0, 2))], axis=1).astype(jnp.float32)
        scores = jnp.einsum('qhgd,hkd->hgqk', query_block, all_keys) * scale_factor
        has_prior = jnp.broadcast_to(block_index >= 1, (QB, QB))
        visible = jnp.concatenate([jnp.ones((QB, SEL * TILE), dtype=bool), has_prior, causal], axis=1)
        masked = jnp.where(visible, scores, NEG_FILL)
        row_top = lax.optimization_barrier(jnp.max(masked, axis=3, keepdims=True))
        exponent = jnp.exp(masked - row_top)
        row_total = lax.optimization_barrier(jnp.sum(exponent, axis=3))
        weights = lax.optimization_barrier(exponent.astype(jnp.bfloat16)).astype(jnp.float32)
        weighted = jnp.einsum('hgqk,hkd->qhgd', weights, all_values)
        result = weighted / jnp.transpose(row_total, (2, 0, 1))[..., None]
        return result.astype(jnp.bfloat16).reshape(QB, HQ * HD)
    return lax.map(one_block, jnp.arange(NQB)).reshape(PROMPT, HQ * HD)
```

```python
import functools
import math

import jax
import jax.numpy as jnp
from jax import lax
from jax.experimental import pallas as pl
from jax.experimental.pallas import tpu as pltpu
from jax.sharding import PartitionSpec as P

HQ = 32
KV = 8
HD = 128
QB = 128
TILE = 128
SEL = 12
RANKS = 2
GROUP = HQ // KV
NEG_FILL = -1e30
VMEM_LIMIT = 50 * 1024 * 1024


def swap_heads(rows, n_head, me):
    if n_head != 2:
        return lax.all_to_all(rows, "head", split_axis=1, concat_axis=0, tiled=True)
    width = rows.shape[1] // 2
    kept = lax.dynamic_slice_in_dim(rows, me * width, width, 1)
    sent = lax.dynamic_slice_in_dim(rows, (1 - me) * width, width, 1)
    got = lax.ppermute(sent, "head", [(0, 1), (1, 0)])
    return jnp.where(
        me == 0, jnp.concatenate([kept, got], axis=0), jnp.concatenate([got, kept], axis=0)
    )


def swap_back(outs, n_head, me):
    width = sum(o.shape[1] for o in outs)
    rows = outs[0].shape[0] // n_head
    if n_head != 2:
        whole = jnp.concatenate(outs, axis=1)
        return lax.all_to_all(whole, "head", split_axis=0, concat_axis=1, tiled=True)
    result = jnp.zeros((rows, 2 * width), outs[0].dtype)
    at = 0
    for o in outs:
        kept = lax.dynamic_slice_in_dim(o, me * rows, rows, 0)
        sent = lax.dynamic_slice_in_dim(o, (1 - me) * rows, rows, 0)
        got = lax.ppermute(sent, "head", [(0, 1), (1, 0)])
        result = lax.dynamic_update_slice(result, kept, (0, me * width + at))
        result = lax.dynamic_update_slice(result, got, (0, (1 - me) * width + at))
        at += o.shape[1]
    return result


def gather_kernel(first, heads, asked, keys, values, out, sem):
    shards = out.shape[0]

    def one(i, carry):
        peer = i // (heads * RANKS)
        rest = i % (heads * RANKS)
        head = rest // RANKS
        rank = rest % RANKS
        tile = asked[peer, (first + head) * RANKS + rank]
        rows = pl.ds(pl.multiple_of(tile * TILE, TILE), TILE)
        cols = pl.ds(pl.multiple_of((first + head) * HD, HD), HD)
        pltpu.make_async_copy(keys.at[rows, cols], out.at[peer, head, rank, 0], sem).start()
        pltpu.make_async_copy(values.at[rows, cols], out.at[peer, head, rank, 1], sem).start()
        return carry

    lax.fori_loop(0, shards * heads * RANKS, one, 0)
    pltpu.make_async_copy(out, out, sem).wait()


def gather_tiles(asked, keys, values, first, heads):
    shards = asked.shape[0]
    shape = (shards, heads, RANKS, 2, TILE, HD)
    return pl.pallas_call(
        functools.partial(gather_kernel, first, heads),
        out_shape=jax.ShapeDtypeStruct(shape, jnp.bfloat16),
        grid_spec=pltpu.PrefetchScalarGridSpec(
            num_scalar_prefetch=1,
            grid=(),
            in_specs=[pl.BlockSpec(memory_space=pl.ANY)] * 2,
            out_specs=pl.BlockSpec(memory_space=pl.ANY),
            scratch_shapes=[pltpu.SemaphoreType.DMA],
        ),
        cost_estimate=pl.CostEstimate(
            flops=0, bytes_accessed=4 * math.prod(shape), transcendentals=0
        ),
        name="gather_tiles",
    )(asked, keys, values)


def attend_kernel(
    first, slots, info, q_ref, tiles, k_rows, v_rows, k_prior, v_prior, out, k_all, v_all
):
    head = pl.program_id(0)
    block = pl.program_id(1)
    blocks = pl.num_programs(1)
    listed = SEL * TILE
    for j in range(SEL):
        slot = slots[((first + head) * blocks + block) * SEL + j]
        owner = slot // RANKS
        rank = slot % RANKS
        k_all[j * TILE : (j + 1) * TILE, :] = tiles[owner, 0, rank, 0]
        v_all[j * TILE : (j + 1) * TILE, :] = tiles[owner, 0, rank, 1]
    here = pl.ds(pl.multiple_of(block * QB, QB), QB)
    before = pl.ds(pl.multiple_of(jnp.maximum(block - 1, 0) * QB, QB), QB)

    @pl.when(block == 0)
    def _():
        k_all[listed : listed + QB, :] = k_prior[...]
        v_all[listed : listed + QB, :] = v_prior[...]

    @pl.when(block > 0)
    def _():
        k_all[listed : listed + QB, :] = k_rows[before, :]
        v_all[listed : listed + QB, :] = v_rows[before, :]

    k_all[listed + QB :, :] = k_rows[here, :]
    v_all[listed + QB :, :] = v_rows[here, :]
    has_prior = (block > 0) | (info[0] > 0)
    scale = 1.0 / math.sqrt(HD)
    causal = lax.broadcasted_iota(jnp.int32, (QB, QB), 0) >= lax.broadcasted_iota(
        jnp.int32, (QB, QB), 1
    )
    for g in range(GROUP):
        q = q_ref[:, g * HD : (g + 1) * HD]
        s = lax.dot_general(
            q, k_all[...], (((1,), (1,)), ((), ())), preferred_element_type=jnp.float32
        )
        far = s[:, :listed]
        prior = jnp.where(has_prior, s[:, listed : listed + QB], NEG_FILL)
        own = jnp.where(causal, s[:, listed + QB :], NEG_FILL)
        s = jnp.concatenate([far, prior, own], axis=1)
        top = jnp.max(s, axis=1, keepdims=True)
        e = jnp.exp((s - top) * scale)
        total = jnp.sum(e, axis=1, keepdims=True)
        o = jnp.dot(e.astype(jnp.bfloat16), v_all[...], preferred_element_type=jnp.float32)
        out[:, g * HD : (g + 1) * HD] = (o / total).astype(jnp.bfloat16)


def attend(slots, info, q_rows, tiles, k_rows, v_rows, k_prior, v_prior, first):
    rows = q_rows.shape[0]
    blocks = rows // QB
    shards, heads = tiles.shape[:2]
    wide = GROUP * HD
    keys = (SEL + 2) * TILE
    return pl.pallas_call(
        functools.partial(attend_kernel, first),
        out_shape=jax.ShapeDtypeStruct((rows, heads * wide), jnp.bfloat16),
        grid_spec=pltpu.PrefetchScalarGridSpec(
            num_scalar_prefetch=2,
            grid=(heads, blocks),
            in_specs=[
                pl.BlockSpec((QB, wide), lambda h, b, *_: (b, first + h)),
                pl.BlockSpec(
                    (shards, 1, RANKS, 2, TILE, HD), lambda h, b, *_: (0, h, 0, 0, 0, 0)
                ),
                pl.BlockSpec((rows, HD), lambda h, b, *_: (0, first + h)),
                pl.BlockSpec((rows, HD), lambda h, b, *_: (0, first + h)),
                pl.BlockSpec((QB, HD), lambda h, b, *_: (0, first + h)),
                pl.BlockSpec((QB, HD), lambda h, b, *_: (0, first + h)),
            ],
            out_specs=pl.BlockSpec((QB, wide), lambda h, b, *_: (b, h)),
            scratch_shapes=[pltpu.VMEM((keys, HD), jnp.bfloat16)] * 2,
        ),
        compiler_params=pltpu.CompilerParams(vmem_limit_bytes=VMEM_LIMIT),
        cost_estimate=pl.CostEstimate(
            flops=4 * heads * rows * GROUP * keys * HD,
            bytes_accessed=2 * math.prod(tiles.shape),
            transcendentals=heads * rows * GROUP * keys,
        ),
        name="attend",
    )(slots, info, q_rows, tiles, k_rows, v_rows, k_prior, v_prior)


def on_device(queries, new_keys, new_values, cache_keys, cache_values, tile_lists):
    shards = lax.axis_size("seq")
    n_head = lax.axis_size("head")
    shard = lax.axis_index("seq")
    me = lax.axis_index("head")
    blocks, kv_here, _ = tile_lists.shape
    tiles_here = cache_keys.shape[0] // TILE

    listed = jnp.transpose(tile_lists, (1, 0, 2)).reshape(kv_here, blocks * SEL)
    local = listed % tiles_here
    match = (listed // tiles_here)[None] == jnp.arange(shards)[:, None, None]
    low = jnp.min(jnp.where(match, local[None], tiles_here - 1), axis=2)
    high = jnp.max(jnp.where(match, local[None], 0), axis=2)
    wanted = jnp.stack([low, high], axis=2).reshape(shards, kv_here * RANKS)
    asked = lax.all_to_all(wanted, "seq", split_axis=0, concat_axis=0, tiled=True)
    rank = jnp.any(match & (local[None] != low[:, :, None]), axis=0)
    slots = (listed // tiles_here * RANKS + rank).reshape(-1)
    info = jnp.reshape(shard, (1,))

    cut = max(1, kv_here - 1)
    parts = [(0, cut), (cut, kv_here - cut)] if kv_here > 1 else [(0, 1)]
    got = []
    for first, heads in parts:
        sent = gather_tiles(asked, cache_keys, cache_values, first, heads)
        got.append(lax.all_to_all(sent, "seq", split_axis=0, concat_axis=0, tiled=True))

    q_rows = swap_heads(queries, n_head, me)
    k_rows = swap_heads(new_keys, n_head, me)
    v_rows = swap_heads(new_values, n_head, me)
    route = [(i, i + 1) for i in range(shards - 1)]
    k_prior, v_prior = lax.ppermute((k_rows[-QB:], v_rows[-QB:]), "seq", route)

    outs = [
        attend(slots, info, q_rows, tiles, k_rows, v_rows, k_prior, v_prior, first)
        for (first, _), tiles in zip(parts, got)
    ]
    return swap_back(outs, n_head, me)


def solution(mesh):
    return jax.shard_map(
        on_device,
        mesh=mesh,
        in_specs=(
            P(("seq", "head"), None),
            P(("seq", "head"), None),
            P(("seq", "head"), None),
            P("seq", "head"),
            P("seq", "head"),
            P("seq", "head", None),
        ),
        out_specs=P(("seq", "head"), None),
        check_vma=False,
    )
```

```python
import functools
import math

import jax
import jax.numpy as jnp
from jax import lax
from jax.experimental import pallas as pl
from jax.experimental.pallas import tpu as pltpu
from jax.sharding import PartitionSpec as P

HQ = 32
KV = 8
HD = 128
QB = 128
TILE = 128
SEL = 12
RANKS = 2
GROUP = HQ // KV
NEG_FILL = -1e30
VMEM_LIMIT = 50 * 1024 * 1024


def swap_heads(rows, n_head, me):
    if n_head != 2:
        return lax.all_to_all(rows, "head", split_axis=1, concat_axis=0, tiled=True)
    width = rows.shape[1] // 2
    kept = lax.dynamic_slice_in_dim(rows, me * width, width, 1)
    sent = lax.dynamic_slice_in_dim(rows, (1 - me) * width, width, 1)
    got = lax.ppermute(sent, "head", [(0, 1), (1, 0)])
    return jnp.where(
        me == 0, jnp.concatenate([kept, got], axis=0), jnp.concatenate([got, kept], axis=0)
    )


def swap_back(outs, n_head, me):
    width = sum(o.shape[1] for o in outs)
    rows = outs[0].shape[0] // n_head
    if n_head != 2:
        whole = jnp.concatenate(outs, axis=1)
        return lax.all_to_all(whole, "head", split_axis=0, concat_axis=1, tiled=True)
    result = jnp.zeros((rows, 2 * width), outs[0].dtype)
    at = 0
    for o in outs:
        kept = lax.dynamic_slice_in_dim(o, me * rows, rows, 0)
        sent = lax.dynamic_slice_in_dim(o, (1 - me) * rows, rows, 0)
        got = lax.ppermute(sent, "head", [(0, 1), (1, 0)])
        result = lax.dynamic_update_slice(result, kept, (0, me * width + at))
        result = lax.dynamic_update_slice(result, got, (0, (1 - me) * width + at))
        at += o.shape[1]
    return result


def gather_kernel(first, heads, asked, keys, values, out, held, load_sem, sem):
    shards = out.shape[0]
    loads = []
    for head in range(heads):
        cols = pl.ds((first + head) * HD, HD)
        for kind, source in enumerate((keys, values)):
            load = pltpu.make_async_copy(
                source.at[:, cols], held.at[head, kind], load_sem.at[head, kind]
            )
            load.start()
            loads.append(load)
    for head in range(heads):
        loads[2 * head].wait()
        loads[2 * head + 1].wait()

        def one(i, carry, head=head):
            peer = i // RANKS
            rank = i % RANKS
            tile = asked[peer, (first + head) * RANKS + rank]
            rows = pl.ds(pl.multiple_of(tile * TILE, TILE), TILE)
            pltpu.make_async_copy(
                held.at[head, :, rows], out.at[peer, head, rank], sem
            ).start()
            return carry

        lax.fori_loop(0, shards * RANKS, one, 0, unroll=4)
    pltpu.make_async_copy(out, out, sem).wait()


def gather_tiles(asked, keys, values, first, heads):
    shards = asked.shape[0]
    shape = (shards, heads, RANKS, 2, TILE, HD)
    return pl.pallas_call(
        functools.partial(gather_kernel, first, heads),
        out_shape=jax.ShapeDtypeStruct(shape, jnp.bfloat16),
        grid_spec=pltpu.PrefetchScalarGridSpec(
            num_scalar_prefetch=1,
            grid=(),
            in_specs=[pl.BlockSpec(memory_space=pl.ANY)] * 2,
            out_specs=pl.BlockSpec(memory_space=pl.ANY),
            scratch_shapes=[
                pltpu.VMEM((heads, 2, keys.shape[0], HD), jnp.bfloat16),
                pltpu.SemaphoreType.DMA((heads, 2)),
                pltpu.SemaphoreType.DMA,
            ],
        ),
        compiler_params=pltpu.CompilerParams(vmem_limit_bytes=VMEM_LIMIT),
        cost_estimate=pl.CostEstimate(
            flops=0, bytes_accessed=4 * math.prod(shape), transcendentals=0
        ),
        name="gather_tiles",
    )(asked, keys, values)


def attend_kernel(
    first, slots, info, q_ref, tiles, k_rows, v_rows, k_prior, v_prior, out, k_all, v_all
):
    head = pl.program_id(0)
    block = pl.program_id(1)
    blocks = pl.num_programs(1)
    listed = SEL * TILE
    for j in range(SEL):
        slot = slots[((first + head) * blocks + block) * SEL + j]
        owner = slot // RANKS
        rank = slot % RANKS
        k_all[j * TILE : (j + 1) * TILE, :] = tiles[owner, 0, rank, 0]
        v_all[j * TILE : (j + 1) * TILE, :] = tiles[owner, 0, rank, 1]
    here = pl.ds(pl.multiple_of(block * QB, QB), QB)
    before = pl.ds(pl.multiple_of(jnp.maximum(block - 1, 0) * QB, QB), QB)

    @pl.when(block == 0)
    def _():
        k_all[listed : listed + QB, :] = k_prior[...]
        v_all[listed : listed + QB, :] = v_prior[...]

    @pl.when(block > 0)
    def _():
        k_all[listed : listed + QB, :] = k_rows[before, :]
        v_all[listed : listed + QB, :] = v_rows[before, :]

    k_all[listed + QB :, :] = k_rows[here, :]
    v_all[listed + QB :, :] = v_rows[here, :]
    has_prior = (block > 0) | (info[0] > 0)
    scale = 1.0 / math.sqrt(HD)
    causal = lax.broadcasted_iota(jnp.int32, (QB, QB), 0) >= lax.broadcasted_iota(
        jnp.int32, (QB, QB), 1
    )
    for g in range(GROUP):
        q = q_ref[:, g * HD : (g + 1) * HD]
        s = lax.dot_general(
            q, k_all[...], (((1,), (1,)), ((), ())), preferred_element_type=jnp.float32
        )
        far = s[:, :listed]
        prior = jnp.where(has_prior, s[:, listed : listed + QB], NEG_FILL)
        own = jnp.where(causal, s[:, listed + QB :], NEG_FILL)
        s = jnp.concatenate([far, prior, own], axis=1)
        top = jnp.max(s, axis=1, keepdims=True)
        e = jnp.exp((s - top) * scale)
        total = jnp.sum(e, axis=1, keepdims=True)
        o = jnp.dot(e.astype(jnp.bfloat16), v_all[...], preferred_element_type=jnp.float32)
        out[:, g * HD : (g + 1) * HD] = (o / total).astype(jnp.bfloat16)


def attend(slots, info, q_rows, tiles, k_rows, v_rows, k_prior, v_prior, first):
    rows = q_rows.shape[0]
    blocks = rows // QB
    shards, heads = tiles.shape[:2]
    wide = GROUP * HD
    keys = (SEL + 2) * TILE
    return pl.pallas_call(
        functools.partial(attend_kernel, first),
        out_shape=jax.ShapeDtypeStruct((rows, heads * wide), jnp.bfloat16),
        grid_spec=pltpu.PrefetchScalarGridSpec(
            num_scalar_prefetch=2,
            grid=(heads, blocks),
            in_specs=[
                pl.BlockSpec((QB, wide), lambda h, b, *_: (b, first + h)),
                pl.BlockSpec(
                    (shards, 1, RANKS, 2, TILE, HD), lambda h, b, *_: (0, h, 0, 0, 0, 0)
                ),
                pl.BlockSpec((rows, HD), lambda h, b, *_: (0, first + h)),
                pl.BlockSpec((rows, HD), lambda h, b, *_: (0, first + h)),
                pl.BlockSpec((QB, HD), lambda h, b, *_: (0, first + h)),
                pl.BlockSpec((QB, HD), lambda h, b, *_: (0, first + h)),
            ],
            out_specs=pl.BlockSpec((QB, wide), lambda h, b, *_: (b, h)),
            scratch_shapes=[pltpu.VMEM((keys, HD), jnp.bfloat16)] * 2,
        ),
        compiler_params=pltpu.CompilerParams(vmem_limit_bytes=VMEM_LIMIT),
        cost_estimate=pl.CostEstimate(
            flops=4 * heads * rows * GROUP * keys * HD,
            bytes_accessed=2 * math.prod(tiles.shape),
            transcendentals=heads * rows * GROUP * keys,
        ),
        name="attend",
    )(slots, info, q_rows, tiles, k_rows, v_rows, k_prior, v_prior)


def on_device(queries, new_keys, new_values, cache_keys, cache_values, tile_lists):
    shards = lax.axis_size("seq")
    n_head = lax.axis_size("head")
    shard = lax.axis_index("seq")
    me = lax.axis_index("head")
    blocks, kv_here, _ = tile_lists.shape
    tiles_here = cache_keys.shape[0] // TILE

    listed = jnp.transpose(tile_lists, (1, 0, 2)).reshape(kv_here, blocks * SEL)
    local = listed % tiles_here
    match = (listed // tiles_here)[None] == jnp.arange(shards)[:, None, None]
    low = jnp.min(jnp.where(match, local[None], tiles_here - 1), axis=2)
    high = jnp.max(jnp.where(match, local[None], 0), axis=2)
    wanted = jnp.stack([low, high], axis=2).reshape(shards, kv_here * RANKS)
    asked = lax.all_to_all(wanted, "seq", split_axis=0, concat_axis=0, tiled=True)
    rank = jnp.any(match & (local[None] != low[:, :, None]), axis=0)
    slots = (listed // tiles_here * RANKS + rank).reshape(-1)
    info = jnp.reshape(shard, (1,))

    q_rows = swap_heads(queries, n_head, me)
    k_rows = swap_heads(new_keys, n_head, me)
    v_rows = swap_heads(new_values, n_head, me)
    route = [(i, i + 1) for i in range(shards - 1)]
    k_prior, v_prior = lax.ppermute((k_rows[-QB:], v_rows[-QB:]), "seq", route)

    cut = max(1, kv_here - 1)
    parts = [(0, cut), (cut, kv_here - cut)] if kv_here > 1 else [(0, 1)]
    sent = [gather_tiles(asked, cache_keys, cache_values, *part) for part in parts]
    got = [lax.all_to_all(sent[0], "seq", split_axis=0, concat_axis=0, tiled=True)]
    for later in sent[1:]:
        later, q_rows, k_rows, v_rows, k_prior, v_prior = lax.optimization_barrier(
            (later, q_rows, k_rows, v_rows, k_prior, v_prior)
        )
        got.append(lax.all_to_all(later, "seq", split_axis=0, concat_axis=0, tiled=True))

    outs = [
        attend(slots, info, q_rows, tiles, k_rows, v_rows, k_prior, v_prior, first)
        for (first, _), tiles in zip(parts, got)
    ]
    return swap_back(outs, n_head, me)


def solution(mesh):
    return jax.shard_map(
        on_device,
        mesh=mesh,
        in_specs=(
            P(("seq", "head"), None),
            P(("seq", "head"), None),
            P(("seq", "head"), None),
            P("seq", "head"),
            P("seq", "head"),
            P("seq", "head", None),
        ),
        out_specs=P(("seq", "head"), None),
        check_vma=False,
    )
```

```python
import functools
import math

import jax
import jax.numpy as jnp
from jax import lax
from jax.experimental import pallas as pl
from jax.experimental.pallas import tpu as pltpu
from jax.sharding import PartitionSpec as P

HQ = 32
KV = 8
HD = 128
QB = 128
TILE = 128
SEL = 12
RANKS = 2
GROUP = HQ // KV
NEG_FILL = -1e30
VMEM_LIMIT = 50 * 1024 * 1024

PLACES = 8
CUTS = (4, 6, 7)
HAND = 3
RELAY = 1 << 16
WIDE = 16


def swap_heads(rows, n_head, me):
    if n_head != 2:
        return lax.all_to_all(rows, "head", split_axis=1, concat_axis=0, tiled=True)
    width = rows.shape[1] // 2
    kept = lax.dynamic_slice_in_dim(rows, me * width, width, 1)
    sent = lax.dynamic_slice_in_dim(rows, (1 - me) * width, width, 1)
    got = lax.ppermute(sent, "head", [(0, 1), (1, 0)])
    return jnp.where(
        me == 0, jnp.concatenate([kept, got], axis=0), jnp.concatenate([got, kept], axis=0)
    )


def swap_back(out, n_head, me):
    rows = out.shape[0] // n_head
    kept = lax.dynamic_slice_in_dim(out, me * rows, rows, 0)
    sent = lax.dynamic_slice_in_dim(out, (1 - me) * rows, rows, 0)
    return kept, lax.ppermute(sent, "head", [(0, 1), (1, 0)])


def place_columns(result, kept, got, me, at):
    width = result.shape[1] // 2
    result = lax.dynamic_update_slice(result, kept, (0, me * width + at))
    return lax.dynamic_update_slice(result, got, (0, (1 - me) * width + at))


def attend_block(q_ref, out, k_all, v_all, has_prior):
    listed = SEL * TILE
    scale = 1.0 / math.sqrt(HD)
    causal = lax.broadcasted_iota(jnp.int32, (QB, QB), 0) >= lax.broadcasted_iota(
        jnp.int32, (QB, QB), 1
    )
    for g in range(GROUP):
        q = q_ref[:, g * HD : (g + 1) * HD]
        s = lax.dot_general(
            q, k_all[...], (((1,), (1,)), ((), ())), preferred_element_type=jnp.float32
        )
        far = s[:, :listed]
        prior = jnp.where(has_prior, s[:, listed : listed + QB], NEG_FILL)
        own = jnp.where(causal, s[:, listed + QB :], NEG_FILL)
        s = jnp.concatenate([far, prior, own], axis=1)
        top = jnp.max(s, axis=1, keepdims=True)
        e = jnp.exp((s - top) * scale)
        total = jnp.sum(e, axis=1, keepdims=True)
        o = jnp.dot(e.astype(jnp.bfloat16), v_all[...], preferred_element_type=jnp.float32)
        out[:, g * HD : (g + 1) * HD] = (o / total).astype(jnp.bfloat16)


def local_rows(block, rows, prior, target):
    listed = SEL * TILE
    here = pl.ds(pl.multiple_of(block * QB, QB), QB)
    before = pl.ds(pl.multiple_of(jnp.maximum(block - 1, 0) * QB, QB), QB)

    @pl.when(block == 0)
    def _():
        target[listed : listed + QB, :] = prior[...]

    @pl.when(block > 0)
    def _():
        target[listed : listed + QB, :] = rows[before, :]

    target[listed + QB :, :] = rows[here, :]


def attend_cost(heads, rows, slots):
    keys = (SEL + 2) * TILE
    return pl.CostEstimate(
        flops=4 * heads * rows * GROUP * keys * HD,
        bytes_accessed=2 * slots * 2 * TILE * HD + 4 * heads * rows * GROUP * HD,
        transcendentals=heads * rows * GROUP * keys,
    )


def code_of(lane, place, half):
    lanes = 2 * half
    early, middle = CUTS[0], CUTS[1] - CUTS[0]
    first = lane * early + place
    near = lanes * early + lane * (PLACES - early) + place - early
    far = lanes * early + half * (PLACES - early) + (lane - half) * middle + place - early
    last = lanes * early + half * (PLACES - early + middle) + lane - half
    code = jnp.where(place < CUTS[1], far, last)
    code = jnp.where(lane < half, near, code)
    return jnp.where(place < early, first, code)


def counts_of(half):
    lanes = 2 * half
    first = lanes * CUTS[0]
    second = first + half * (PLACES - CUTS[0] + CUTS[1] - CUTS[0])
    return first, second, second + half


def plan_kernel(tiles_here, low, high, shard, ask, where, spare_where, failed, count, free):
    shards = ask.shape[0]
    heads = low.shape[0] // shards
    half = shards // 2
    me = shard[0]
    extra = counts_of(half)[2]

    def per_owner(o, carry):
        lane = o ^ me
        for p in range(WIDE):
            ask[o, p] = jnp.int32(0)
        place = jnp.int32(0)
        for h in range(heads):
            lo = low[o * heads + h]
            hi = high[o * heads + h]
            for k, (tile, has) in enumerate(((lo, lo <= hi), (hi, lo < hi))):
                ask[o, place] = h * tiles_here + tile
                code = code_of(lane, place, half)
                where[(o * heads + h) * RANKS + k] = code
                spare_where[(o * heads + h) * RANKS + k] = code
                place = place + has.astype(jnp.int32)
        ask[o, PLACES] = jnp.int32(-1)
        count[o] = place
        return carry

    lax.fori_loop(0, shards, per_owner, 0)
    other = jnp.where(me < half, half, 0)
    found = jnp.int32(0)
    for place in range(CUTS[2] - 1, CUTS[0] - 1, -1):

        def look(i, found, place=place):
            o = other + (i + me) % half
            free[found] = o * PLACES + place
            return found + (count[o] <= place).astype(jnp.int32)

        found = lax.fori_loop(0, half, look, found)

    def hand_over(i, used):
        o = other + i
        full = count[o] == PLACES

        @pl.when(full)
        def _():
            at = ((o + 1) * heads - 1) * RANKS + RANKS - 1
            spare_where[at] = extra + o
            where[at] = extra + o

            @pl.when(used < found)
            def _():
                relay = free[used] // PLACES
                place = free[used] % PLACES
                ask[o, PLACES] = relay
                ask[relay, place] = RELAY + o
                where[at] = code_of(relay ^ me, place, half)

        return used + full.astype(jnp.int32)

    used = lax.fori_loop(0, half, hand_over, jnp.int32(0))
    failed[0] = (used > found).astype(jnp.int32)


def make_plan(low, high, shard, tiles_here):
    shards, heads = low.shape
    smem = pl.BlockSpec(memory_space=pltpu.SMEM)
    half = shards // 2
    return pl.pallas_call(
        functools.partial(plan_kernel, tiles_here),
        out_shape=(
            jax.ShapeDtypeStruct((shards, WIDE), jnp.int32),
            jax.ShapeDtypeStruct((shards * heads * RANKS,), jnp.int32),
            jax.ShapeDtypeStruct((shards * heads * RANKS,), jnp.int32),
            jax.ShapeDtypeStruct((1,), jnp.int32),
        ),
        in_specs=[smem] * 3,
        out_specs=(smem,) * 4,
        scratch_shapes=[
            pltpu.SMEM((shards,), jnp.int32),
            pltpu.SMEM(((CUTS[2] - CUTS[0]) * half + 1,), jnp.int32),
        ],
        name="plan",
    )(low.reshape(-1), high.reshape(-1), shard)


def load_cache(keys, values, held, load_sem):
    loads = [
        pltpu.make_async_copy(source, held.at[kind], load_sem.at[kind])
        for kind, source in enumerate((keys, values))
    ]
    for load in loads:
        load.start()
    for load in loads:
        load.wait()


def copy_tile(held, code, tiles_here, target, sem):
    head = code // tiles_here
    tile = code % tiles_here
    rows = pl.ds(pl.multiple_of(tile * TILE, TILE), TILE)
    cols = pl.ds(pl.multiple_of(head * HD, HD), HD)
    pltpu.make_async_copy(held.at[:, rows, cols], target, sem).start()


def first_kernel(half, asked, shard, keys, values, *rest):
    outs, (held, load_sem, sem) = rest[:-3], rest[-3:]
    tiles_here = keys.shape[0] // TILE
    load_cache(keys, values, held, load_sem)
    for i, out in enumerate(outs):
        peer = (half + i) ^ shard[0]
        for p in range(out.shape[0]):
            copy_tile(held, asked[peer, p], tiles_here, out.at[p], sem)
    for out in outs:
        pltpu.make_async_copy(out, out, sem).wait()


def near_kernel(half, asked, shard, keys, values, *rest):
    outs, failed, (held, load_sem, sem, hand, filled) = rest[:-6], rest[-6], rest[-5:]
    near, given = outs[:half], outs[half:]
    tiles_here = keys.shape[0] // TILE
    me = shard[0]
    load_cache(keys, values, held, load_sem)
    for lane, out in enumerate(near):
        peer = lane ^ me
        for p in range(out.shape[0]):
            copy_tile(held, asked[peer, p], tiles_here, out.at[p], sem)
    for lane in range(half):
        filled[lane] = jnp.int32(0)
        for f in range(HAND + 1):
            hand[lane * (HAND + 1) + f] = jnp.int32(0)
    other = jnp.where(me < half, half, 0)

    def look(i, over):
        relay = asked[other + i, PLACES]
        lane = jnp.where(relay >= 0, relay ^ me, 0)
        at = jnp.minimum(filled[lane], HAND)
        hand[lane * (HAND + 1) + at] = asked[other + i, PLACES - 1]
        filled[lane] = filled[lane] + 1
        return over | ((relay >= 0) & (at == HAND)).astype(jnp.int32)

    failed[0] = lax.fori_loop(0, half, look, jnp.int32(0))
    for i, out in enumerate(given):
        for f in range(HAND):
            copy_tile(held, hand[(i + 1) * (HAND + 1) + f], tiles_here, out.at[f], sem)
    for out in outs:
        pltpu.make_async_copy(out, out, sem).wait()


def rest_kernel(half, asked, shard, keys, values, *rest):
    given, rest = rest[: half - 1], rest[half - 1 :]
    outs, (held, relayed, load_sem, sem, filled, source) = rest[:-6], rest[-6:]
    tiles_here = keys.shape[0] // TILE
    me = shard[0]
    loads = []
    for i, array in enumerate(given):
        load = pltpu.make_async_copy(array, relayed.at[i + 1], load_sem.at[2])
        load.start()
        loads.append(load)
    load_cache(keys, values, held, load_sem)
    for load in loads:
        load.wait()
    places = range(CUTS[0], CUTS[2])
    for lane in range(half):
        filled[lane] = jnp.int32(0)
    other = jnp.where(me < half, half, 0)

    def look(i, carry):
        for q, p in enumerate(places):
            code = asked[other + i, p]
            is_relay = code >= RELAY
            lane = jnp.where(is_relay, (code - RELAY) ^ me, 0)
            slot = jnp.minimum(filled[lane], HAND - 1)
            source[i * len(places) + q] = jnp.where(is_relay, RELAY + lane * HAND + slot, code)
            filled[lane] = filled[lane] + 1
        return carry

    lax.fori_loop(0, half, look, 0)
    for i in range(half):
        to = ((half + i) ^ me) - other
        for q, p in enumerate(places):
            second = p >= CUTS[1]
            out = outs[half + i].at[p - CUTS[1]] if second else outs[i].at[p - CUTS[0]]
            code = source[to * len(places) + q]

            @pl.when(code >= RELAY)
            def _():
                at = code - RELAY
                pltpu.make_async_copy(relayed.at[at // HAND, at % HAND], out, sem).start()

            @pl.when(code < RELAY)
            def _():
                copy_tile(held, code, tiles_here, out, sem)

    for out in outs:
        pltpu.make_async_copy(out, out, sem).wait()


def extra_kernel(asked, keys, values, out, held, load_sem, sem):
    tiles_here = keys.shape[0] // TILE
    load_cache(keys, values, held, load_sem)
    for i in range(out.shape[0]):
        copy_tile(held, asked[i, PLACES - 1], tiles_here, out.at[i], sem)
    pltpu.make_async_copy(out, out, sem).wait()


def gather_call(kernel, name, tables, keys, values, more, counts, flag=False, scratch=()):
    hbm = pl.BlockSpec(memory_space=pl.ANY)
    shapes = [jax.ShapeDtypeStruct((n, 2, TILE, HD), jnp.bfloat16) for n in counts]
    specs = [hbm] * len(counts)
    if flag:
        shapes.append(jax.ShapeDtypeStruct((1,), jnp.int32))
        specs.append(pl.BlockSpec(memory_space=pltpu.SMEM))
    return pl.pallas_call(
        kernel,
        out_shape=shapes,
        grid_spec=pltpu.PrefetchScalarGridSpec(
            num_scalar_prefetch=len(tables),
            grid=(),
            in_specs=[hbm] * (2 + len(more)),
            out_specs=specs,
            scratch_shapes=[pltpu.VMEM((2, *keys.shape), jnp.bfloat16), *scratch],
        ),
        compiler_params=pltpu.CompilerParams(vmem_limit_bytes=VMEM_LIMIT),
        cost_estimate=pl.CostEstimate(
            flops=0,
            bytes_accessed=4 * keys.size + 4 * sum(counts) * TILE * HD * 2,
            transcendentals=0,
        ),
        name=name,
    )(*tables, keys, values, *more)


def attend_kernel(stages, flagged, first, keep, slots, info, picks, *refs):
    q_ref, k_rows, v_rows, k_prior, v_prior = refs[:5]
    staged, k_all, v_all, sem = refs[-4:]
    arrays = refs[5 : -5 - (1 if keep else 0)]
    out = refs[-5 - (1 if keep else 0)]
    head = pl.program_id(0)
    block = pl.program_id(1)
    blocks = pl.num_programs(1)

    @pl.when((head == 0) & (block == 0))
    def _():
        copies = [
            pltpu.make_async_copy(
                arrays[i].at[pl.ds(start, count)], staged.at[pl.ds(to, count)], sem
            )
            for i, start, count, to in stages
        ]
        for copy in copies:
            copy.start()
        for copy in copies:
            copy.wait()
        if flagged is not None:
            i, to = flagged

            @pl.when(info[1] > 0)
            def _():
                copy = pltpu.make_async_copy(
                    arrays[i], staged.at[pl.ds(to, arrays[i].shape[0])], sem
                )
                copy.start()
                copy.wait()

        if keep:
            kept = refs[-5]
            for i in range(keep):
                pltpu.make_async_copy(staged.at[picks[i]], kept.at[i], sem).start()

    for j in range(SEL):
        slot = slots[((first + head) * blocks + block) * SEL + j]
        k_all[j * TILE : (j + 1) * TILE, :] = staged[slot, 0]
        v_all[j * TILE : (j + 1) * TILE, :] = staged[slot, 1]
    local_rows(block, k_rows, k_prior, k_all)
    local_rows(block, v_rows, v_prior, v_all)
    attend_block(q_ref, out, k_all, v_all, (block > 0) | (info[0] > 0))

    if keep:

        @pl.when((head == pl.num_programs(0) - 1) & (block == blocks - 1))
        def _():
            pltpu.make_async_copy(refs[-5], refs[-5], sem).wait()


def attend(slots, info, picks, q_rows, k_rows, v_rows, k_prior, v_prior, pieces, first, heads,
           flagged=None, keep=0):
    rows = q_rows.shape[0]
    blocks = rows // QB
    wide = GROUP * HD
    keys = (SEL + 2) * TILE
    arrays, stages = [], []
    for array, start, count, to in pieces:
        at = [i for i, other in enumerate(arrays) if other is array]
        if not at:
            at = [len(arrays)]
            arrays.append(array)
        stages.append((at[0], start, count, to))
    size = max(to + count for _, _, count, to in stages)
    if flagged is not None:
        array, to = flagged
        flagged = (len(arrays), to)
        arrays.append(array)
        size = max(size, to + array.shape[0])
    hbm = pl.BlockSpec(memory_space=pl.ANY)
    shapes = [jax.ShapeDtypeStruct((rows, heads * wide), jnp.bfloat16)]
    specs = [pl.BlockSpec((QB, wide), lambda h, b, *_: (b, h))]
    if keep:
        shapes.append(jax.ShapeDtypeStruct((keep, 2, TILE, HD), jnp.bfloat16))
        specs.append(hbm)
    return pl.pallas_call(
        functools.partial(attend_kernel, stages, flagged, first, keep),
        out_shape=shapes,
        grid_spec=pltpu.PrefetchScalarGridSpec(
            num_scalar_prefetch=3,
            grid=(heads, blocks),
            in_specs=[
                pl.BlockSpec((QB, wide), lambda h, b, *_: (b, first + h)),
                pl.BlockSpec((rows, HD), lambda h, b, *_: (0, first + h)),
                pl.BlockSpec((rows, HD), lambda h, b, *_: (0, first + h)),
                pl.BlockSpec((QB, HD), lambda h, b, *_: (0, first + h)),
                pl.BlockSpec((QB, HD), lambda h, b, *_: (0, first + h)),
            ]
            + [hbm] * len(arrays),
            out_specs=specs,
            scratch_shapes=[
                pltpu.VMEM((size, 2, TILE, HD), jnp.bfloat16),
                pltpu.VMEM((keys, HD), jnp.bfloat16),
                pltpu.VMEM((keys, HD), jnp.bfloat16),
                pltpu.SemaphoreType.DMA,
            ],
        ),
        compiler_params=pltpu.CompilerParams(vmem_limit_bytes=VMEM_LIMIT),
        cost_estimate=attend_cost(heads, rows, size),
        name="attend",
    )(slots, info, picks, q_rows, k_rows, v_rows, k_prior, v_prior, *arrays)


def requests(tile_lists, shards, tiles_here):
    blocks, kv_here, _ = tile_lists.shape
    listed = jnp.transpose(tile_lists, (1, 0, 2)).reshape(kv_here, blocks * SEL)
    local = listed % tiles_here
    match = (listed // tiles_here)[None] == jnp.arange(shards)[:, None, None]
    low = jnp.min(jnp.where(match, local[None], tiles_here - 1), axis=2)
    high = jnp.max(jnp.where(match, local[None], 0), axis=2)
    second = local[None] != low[:, :, None]
    return match, second, low, high


def slots_of(match, second, codes):
    picked = jnp.where(second, codes[:, :, 1:2], codes[:, :, 0:1])
    return jnp.sum(jnp.where(match, picked, 0), axis=0)


def crossed(arrays, lanes, shards):
    return [
        lax.ppermute(x, "seq", [(i, i ^ lane) for i in range(shards)])
        for x, lane in zip(arrays, lanes)
    ]


def prompt_rows(queries, new_keys, new_values, shards, n_head, me):
    q_rows = swap_heads(queries, n_head, me)
    k_rows = swap_heads(new_keys, n_head, me)
    v_rows = swap_heads(new_values, n_head, me)
    route = [(i, i + 1) for i in range(shards - 1)]
    k_prior, v_prior = lax.ppermute((k_rows[-QB:], v_rows[-QB:]), "seq", route)
    return q_rows, k_rows, v_rows, k_prior, v_prior


def packed(queries, new_keys, new_values, cache_keys, cache_values, tile_lists):
    shards = lax.axis_size("seq")
    n_head = lax.axis_size("head")
    shard = lax.axis_index("seq")
    me = lax.axis_index("head")
    blocks, kv_here, _ = tile_lists.shape
    tiles_here = cache_keys.shape[0] // TILE
    half = shards // 2
    lanes = range(half, shards)
    at = jnp.reshape(shard, (1,))

    match, second, low, high = requests(tile_lists, shards, tiles_here)
    ask, where, spare_where, failed = make_plan(low, high, at, tiles_here)
    asked = lax.all_to_all(ask, "seq", split_axis=0, concat_axis=0, tiled=True)

    dma = pltpu.SemaphoreType.DMA
    early, middle, late = CUTS[0], CUTS[1] - CUTS[0], CUTS[2] - CUTS[1]
    sent = gather_call(
        functools.partial(first_kernel, half), "gather_first", (asked, at),
        cache_keys, cache_values, (), [early] * half, scratch=(dma((3,)), dma),
    )
    got_first = crossed(sent, lanes, shards)
    asked, _ = lax.optimization_barrier((asked, sent[0]))
    *near, failed_here = gather_call(
        functools.partial(near_kernel, half), "gather_near", (asked, at),
        cache_keys, cache_values, (), [PLACES] * half + [HAND] * (half - 1), flag=True,
        scratch=(
            dma((3,)), dma, pltpu.SMEM((half * (HAND + 1),), jnp.int32),
            pltpu.SMEM((half,), jnp.int32),
        ),
    )
    near, given = near[:half], near[half:]
    given = crossed(given, range(1, half), shards)
    near = near[:1] + crossed(near[1:], range(1, half), shards)
    sent = gather_call(
        functools.partial(rest_kernel, half), "gather_rest", (asked, at),
        cache_keys, cache_values, given, [middle] * half + [late] * half,
        scratch=(
            pltpu.VMEM((half, HAND, 2, TILE, HD), jnp.bfloat16), dma((3,)), dma,
            pltpu.SMEM((half,), jnp.int32), pltpu.SMEM((half * (middle + late),), jnp.int32),
        ),
    )
    got_middle = crossed(sent[:half], lanes, shards)
    got_last = crossed(sent[half:], lanes, shards)
    flag = lax.pmax(jnp.maximum(failed, failed_here), ("seq", "head"))

    def send_extra():
        out = gather_call(
            extra_kernel, "gather_extra", (asked,), cache_keys, cache_values, (), [shards],
            scratch=(dma((3,)), dma),
        )[0]
        return lax.all_to_all(out, "seq", split_axis=0, concat_axis=0, tiled=True)

    def no_extra():
        return jnp.zeros((shards, 2, TILE, HD), jnp.bfloat16)

    extra = lax.cond(flag[0] > 0, send_extra, no_extra)

    rows = prompt_rows(queries, new_keys, new_values, shards, n_head, me)
    info = jnp.concatenate([at, flag])
    codes = where.reshape(shards, kv_here, RANKS)
    slots = slots_of(match, second, codes).reshape(-1)
    first_end, second_end, last_end = counts_of(half)
    final = jnp.where(flag[0] > 0, spare_where, where).reshape(codes.shape)
    final = final[:, kv_here - 1]
    kept = jnp.arange(shards * RANKS).reshape(shards, RANKS)
    picks = jnp.clip(final, 0, second_end - 1).reshape(-1)
    final = jnp.where(final < second_end, kept, final - second_end + shards * RANKS)
    final_slots = slots_of(match[:, -1:], second[:, -1:], final[:, None]).reshape(-1)

    pieces = [(x, 0, early, i * early) for i, x in enumerate(near)]
    pieces += [(x, 0, early, (half + i) * early) for i, x in enumerate(got_first)]
    (out_first,) = attend(slots, info, picks, *rows, pieces, 0, 2)
    later = PLACES - early
    pieces += [(x, early, later, first_end + i * later) for i, x in enumerate(near)]
    pieces += [
        (x, 0, middle, first_end + half * later + i * middle) for i, x in enumerate(got_middle)
    ]
    out_middle, held = attend(slots, info, picks, *rows, pieces, 2, 1, keep=shards * RANKS)
    pieces = [(held, 0, shards * RANKS, 0)]
    pieces += [(x, 0, late, shards * RANKS + i * late) for i, x in enumerate(got_last)]
    q_last = rows[0][:, -GROUP * HD :]
    k_last, v_last, kp_last, vp_last = (x[:, -HD:] for x in rows[1:])
    (out_last,) = attend(
        final_slots, info, picks, q_last, k_last, v_last, kp_last, vp_last, pieces, 0, 1,
        flagged=(extra, shards * RANKS + half * late),
    )

    here = out_first.shape[0] // n_head
    result = jnp.zeros((here, HQ * HD), jnp.bfloat16)
    place = 0
    for out in (out_first, out_middle, out_last):
        result = place_columns(result, *swap_back(out, n_head, me), me, place)
        place += out.shape[1]
    return result


def plain_gather_kernel(first, heads, asked, keys, values, out, held, load_sem, sem):
    shards = out.shape[0]
    loads = []
    for head in range(heads):
        cols = pl.ds((first + head) * HD, HD)
        for kind, source in enumerate((keys, values)):
            load = pltpu.make_async_copy(
                source.at[:, cols], held.at[head, kind], load_sem.at[head, kind]
            )
            load.start()
            loads.append(load)
    for head in range(heads):
        loads[2 * head].wait()
        loads[2 * head + 1].wait()

        def one(i, carry, head=head):
            peer = i // RANKS
            rank = i % RANKS
            tile = asked[peer, (first + head) * RANKS + rank]
            rows = pl.ds(pl.multiple_of(tile * TILE, TILE), TILE)
            pltpu.make_async_copy(
                held.at[head, :, rows], out.at[peer, head, rank], sem
            ).start()
            return carry

        lax.fori_loop(0, shards * RANKS, one, 0, unroll=4)
    pltpu.make_async_copy(out, out, sem).wait()


def gather_tiles(asked, keys, values, first, heads):
    shards = asked.shape[0]
    shape = (shards, heads, RANKS, 2, TILE, HD)
    return pl.pallas_call(
        functools.partial(plain_gather_kernel, first, heads),
        out_shape=jax.ShapeDtypeStruct(shape, jnp.bfloat16),
        grid_spec=pltpu.PrefetchScalarGridSpec(
            num_scalar_prefetch=1,
            grid=(),
            in_specs=[pl.BlockSpec(memory_space=pl.ANY)] * 2,
            out_specs=pl.BlockSpec(memory_space=pl.ANY),
            scratch_shapes=[
                pltpu.VMEM((heads, 2, keys.shape[0], HD), jnp.bfloat16),
                pltpu.SemaphoreType.DMA((heads, 2)),
                pltpu.SemaphoreType.DMA,
            ],
        ),
        compiler_params=pltpu.CompilerParams(vmem_limit_bytes=VMEM_LIMIT),
        cost_estimate=pl.CostEstimate(
            flops=0, bytes_accessed=4 * math.prod(shape), transcendentals=0
        ),
        name="gather_tiles",
    )(asked, keys, values)


def plain(queries, new_keys, new_values, cache_keys, cache_values, tile_lists):
    shards = lax.axis_size("seq")
    n_head = lax.axis_size("head")
    shard = lax.axis_index("seq")
    me = lax.axis_index("head")
    blocks, kv_here, _ = tile_lists.shape
    tiles_here = cache_keys.shape[0] // TILE

    match, second, low, high = requests(tile_lists, shards, tiles_here)
    wanted = jnp.stack([low, high], axis=2).reshape(shards, kv_here * RANKS)
    asked = lax.all_to_all(wanted, "seq", split_axis=0, concat_axis=0, tiled=True)
    codes = jnp.arange(shards * RANKS).reshape(shards, 1, RANKS)
    slots = slots_of(match, second, jnp.broadcast_to(codes, (shards, kv_here, RANKS))).reshape(-1)
    rows = prompt_rows(queries, new_keys, new_values, shards, n_head, me)
    info = jnp.concatenate([jnp.reshape(shard, (1,)), jnp.zeros((1,), jnp.int32)])
    picks = jnp.zeros((1,), jnp.int32)
    outs = []
    for head in range(kv_here):
        sent = gather_tiles(asked, cache_keys, cache_values, head, 1)
        got = lax.all_to_all(sent, "seq", split_axis=0, concat_axis=0, tiled=True)
        got = got.reshape(shards * RANKS, 2, TILE, HD)
        outs += attend(
            slots, info, picks, *rows, [(got, 0, shards * RANKS, 0)], head, 1
        )
    whole = jnp.concatenate(outs, axis=1)
    return lax.all_to_all(whole, "head", split_axis=0, concat_axis=1, tiled=True)


def on_device(queries, new_keys, new_values, cache_keys, cache_values, tile_lists):
    shards = lax.axis_size("seq")
    fits = tile_lists.shape[1] * RANKS == PLACES and shards >= 4 and shards & (shards - 1) == 0
    plan = packed if fits and lax.axis_size("head") == 2 else plain
    return plan(queries, new_keys, new_values, cache_keys, cache_values, tile_lists)


def solution(mesh):
    return jax.shard_map(
        on_device,
        mesh=mesh,
        in_specs=(
            P(("seq", "head"), None),
            P(("seq", "head"), None),
            P(("seq", "head"), None),
            P("seq", "head"),
            P("seq", "head"),
            P("seq", "head", None),
        ),
        out_specs=P(("seq", "head"), None),
        check_vma=False,
    )
```
